32 devices in a mesh: groups: 1, ctx: 32 (over z, y, x, core).
Axes of the slice: x: 2, y: 2, z: 4, core: 2. Of those that a mesh axis runs over, the one named last changes fastest.
Arguments:
- hidden: bfloat16 [9216, 5120], P(('groups', 'ctx')), may hold values from -6 to 6
- key_weight: bfloat16 [5120, 512], replicated, may hold values from -0.078125 to 0.078125
- value_weight: bfloat16 [5120, 512], replicated, may hold values from -0.078125 to 0.078125
- key_gain: float32 [128], replicated, may hold values from 0.1 to 1.9
- lengths: int32 [8], P('groups'), may hold values from 1 to 2304, 9216 in all
- dest_rows: int32 [8], P('groups'), may hold values from 0 to 7, each once
- queries: bfloat16 [32, 32, 128], P(('groups', 'ctx')), may hold values from -240 to 240
- new_keys: bfloat16 [32, 4, 128], P(('groups', 'ctx')), may hold values from -6 to 6
- new_values: bfloat16 [32, 4, 128], P(('groups', 'ctx')), may hold values from -6 to 6
Outputs:
- attended: bfloat16 [32, 32, 128], P(('groups', 'ctx'))
The draws below stay inside these ranges and needn't reach their ends.
Inputs may be any that keep to these rules, and one draw needn't show every extreme that they name: The prompts' lengths sum to 9216 and the longest is exactly 2304. `dest_rows`: every decode row receives exactly one prompt.
All inputs are finite; a program needn't handle non-finite values.
Results may differ from the reference program's by a relative error of at most 0.012.
The reference program's roundings to bfloat16 on the way count: a program that leaves them out, or rounds other values in their place, can miss the bound.
Values may be sent and summed in bfloat16 or wider, within the bound.
A program may use at most 64 MiB of HBM per device.

```python
import math
import jax
import jax.numpy as jnp
import numpy as np
from jax import lax

D = 5120
KVH = 4
HD = 128
QPK = 8
STEPS = 4
TOKENS = 9216
ROWS = 8
MOST = 2304


def draw_queries(key, part):
    key = jax.random.fold_in(key, 11)
    base = jnp.clip(jax.random.normal(key, (ROWS * KVH, STEPS * QPK, HD), jnp.float32), -4.0, 4.0)
    return (base * 2.5).astype(jnp.bfloat16)


def shard_levels(key, dims, pieces, least, largest):
    factor_of = 1.0
    for dim, parts in pieces:
        steps = jax.random.uniform(jax.random.fold_in(jax.random.fold_in(key, 6), dim), (parts,), jnp.float32, least / len(pieces), largest / len(pieces))
        factor_of = factor_of * jnp.repeat(jnp.exp(steps), dims[dim] // parts).reshape((-1,) + (1,) * (len(dims) - 1 - dim))
    return factor_of


def length_profile(number_of, total, reach, lean):
    portions = [(1 << 20) // math.isqrt(rank ** lean) + 1 for rank in range(2, number_of + 1)]
    surplus, holding = total - reach - (number_of - 1), [1] * (number_of - 1)
    while surplus > 0:
        movable = [i for i in range(number_of - 1) if holding[i] < reach]
        mass, remaining = sum([portions[i] for i in movable]), surplus
        for i in movable:
            more = min(reach - holding[i], max(1, remaining * portions[i] // mass), surplus)
            holding[i] = holding[i] + more
            surplus = surplus - more
    return np.array([reach] + holding)


def uneven(rng, number_of, total, most, skew):
    if number_of == 2:
        one = jax.random.randint(rng, (), max(1, total - most), min(most, total - 1) + 1)
        return jnp.stack([one, total - one])
    sizes = jnp.asarray(length_profile(number_of, total, most, skew), jnp.int32)
    pairs = (number_of - 1) // 2
    source_of, sink = sizes[1:1 + 2 * pairs:2], sizes[2:2 + 2 * pairs:2]
    room = jnp.minimum(source_of - 1, most - sink)
    passed = jax.random.randint(jax.random.fold_in(rng, 1), (pairs,), 0, 1 << 20) % (room + 1)
    sizes = sizes.at[1:1 + 2 * pairs:2].set(source_of - passed).at[2:2 + 2 * pairs:2].set(sink + passed)
    return sizes[jax.random.permutation(jax.random.fold_in(rng, 2), number_of)]


def bell_draw(own_key, extent, scale, reach, split=(), held_as=jnp.bfloat16):
    result = scale * jax.random.normal(own_key, extent, jnp.float32)
    if split:
        result = result * shard_levels(own_key, extent, split, -0.22, 0.18)
    return jnp.clip(result, -reach, reach).astype(held_as)


def setup_inputs(seed: int = 0, part: int = 0) -> dict:
    key_of = jax.random.split(jax.random.key(seed), 10)
    own_keys = jax.random.split(jax.random.fold_in(key_of[9], part), 10)
    hidden = bell_draw(own_keys[0], (TOKENS, D), 1.0, 6.0, ((0, 32),))
    key_weight = bell_draw(key_of[1], (D, KVH * HD), D ** -0.5, 0.078125)
    value_weight = bell_draw(key_of[2], (D, KVH * HD), D ** -0.5, 0.078125)
    key_gain = jnp.clip(1.0 + 0.18 * jax.random.normal(key_of[3], (HD,), jnp.float32), 0.1, 1.9)
    lengths = uneven(own_keys[4], ROWS, TOKENS, MOST, 2).astype(jnp.int32)
    dest_rows = jax.random.permutation(own_keys[5], ROWS).astype(jnp.int32)
    queries = draw_queries(jax.random.fold_in(jax.random.fold_in(key_of[9], part), 71), part)
    new_keys = bell_draw(own_keys[7], (ROWS * KVH, STEPS, HD), 1.5, 6.0, ((0, 32),))
    new_values = bell_draw(own_keys[8], (ROWS * KVH, STEPS, HD), 1.0, 6.0, ((0, 32),))
    return dict(hidden=hidden, key_weight=key_weight, value_weight=value_weight, key_gain=key_gain, lengths=lengths, dest_rows=dest_rows, queries=queries, new_keys=new_keys, new_values=new_values)


ROPE_BASE = 1000000.0
EPS = 1e-06
NEG = -1e+30

def rotate(normed, positions):
    half = normed.shape[-1] // 2
    freq = ROPE_BASE ** (-2.0 * jnp.arange(half, dtype=jnp.float32) / normed.shape[-1])
    angle = positions.astype(jnp.float32)[:, None] * freq[None, :]
    cosine = jnp.cos(angle)[:, None, :]
    sine = jnp.sin(angle)[:, None, :]
    first = normed[..., :half]
    second = normed[..., half:]
    return jnp.concatenate([first * cosine - second * sine, second * cosine + first * sine], -1)

def prompt_tables(lengths, dest_rows):
    ends = jnp.cumsum(lengths).astype(jnp.int32)
    starts = (ends - lengths).astype(jnp.int32)
    prompts = jnp.arange(lengths.shape[0], dtype=jnp.int32)
    owner = lax.optimization_barrier(jnp.sum(jnp.where(dest_rows[None, :] == prompts[:, None], prompts[None, :], 0), 1)).astype(jnp.int32)
    return (starts, ends, owner)

def attend(query, cache_keys, cache_values, live, fresh_keys, fresh_values):
    scale = 1.0 / HD ** 0.5
    far = jnp.dot(query, cache_keys.T, preferred_element_type=jnp.float32) * scale
    far = jnp.where(live[None, :], far, NEG)
    near = jnp.dot(query, fresh_keys.T, preferred_element_type=jnp.float32) * scale
    step_of = jnp.arange(query.shape[0], dtype=jnp.int32) // QPK
    allowed = jnp.arange(fresh_keys.shape[0], dtype=jnp.int32)[None, :] <= step_of[:, None]
    near = jnp.where(allowed, near, NEG)
    top = jnp.maximum(lax.optimization_barrier(jnp.max(far, -1)), lax.optimization_barrier(jnp.max(near, -1)))[:, None]
    far_weights = jnp.where(live[None, :], jnp.exp(far - top), 0.0)
    near_weights = jnp.where(allowed, jnp.exp(near - top), 0.0)
    total = lax.optimization_barrier(jnp.sum(far_weights, -1)) + lax.optimization_barrier(jnp.sum(near_weights, -1))
    mixed = jnp.dot(far_weights.astype(jnp.bfloat16), cache_values, preferred_element_type=jnp.float32)
    mixed = mixed + jnp.dot(near_weights.astype(jnp.bfloat16), fresh_values, preferred_element_type=jnp.float32)
    return (mixed / total[:, None]).astype(jnp.bfloat16)

def reference(hidden, key_weight, value_weight, key_gain, lengths, dest_rows, queries, new_keys, new_values):
    starts, ends, owner = prompt_tables(lengths, dest_rows)
    stream = jnp.arange(TOKENS, dtype=jnp.int32)
    prompt_of = lax.optimization_barrier(jnp.sum((stream[:, None] >= ends[None, :]).astype(jnp.int32), 1))
    prompts = jnp.arange(ROWS, dtype=jnp.int32)
    onehot = prompt_of[:, None] == prompts[None, :]
    positions = stream - lax.optimization_barrier(jnp.sum(jnp.where(onehot, starts[None, :], 0), 1)).astype(jnp.int32)
    raw = jnp.dot(hidden, key_weight, preferred_element_type=jnp.float32).reshape(TOKENS, KVH, HD)
    normed = raw * lax.rsqrt(lax.optimization_barrier(jnp.mean(raw * raw, -1, keepdims=True)) + EPS) * key_gain
    keys = rotate(normed, positions).astype(jnp.bfloat16)
    values = jnp.dot(hidden, value_weight, preferred_element_type=jnp.float32).astype(jnp.bfloat16).reshape(TOKENS, KVH, HD)
    padded_keys = jnp.concatenate([keys, jnp.zeros((MOST, KVH, HD), jnp.bfloat16)], 0)
    padded_values = jnp.concatenate([values, jnp.zeros((MOST, KVH, HD), jnp.bfloat16)], 0)

    def one_slot(slot):
        row = slot // KVH
        head = slot % KVH
        prompt = owner[row]
        start = starts[prompt].astype(jnp.int32)
        length = lengths[prompt]
        zero = jnp.int32(0)
        cache_keys = lax.dynamic_slice(padded_keys, (start, head, zero), (MOST, 1, HD))[:, 0]
        cache_values = lax.dynamic_slice(padded_values, (start, head, zero), (MOST, 1, HD))[:, 0]
        live = jnp.arange(MOST, dtype=jnp.int32) < length
        return attend(queries[slot], cache_keys, cache_values, live, new_keys[slot], new_values[slot])
    return lax.map(one_slot, jnp.arange(ROWS * KVH, dtype=jnp.int32))
```

```python
import functools

import jax
import jax.numpy as jnp
import numpy as np
from jax import lax
from jax.experimental import pallas as pl
from jax.experimental.pallas import tpu as pltpu
from jax.sharding import PartitionSpec as P

KVH = 4
HD = 128
QPK = 8
LANES = 128

ROPE_BASE = 1000000.0
EPS = 1e-06
NEG = -1e30
MESH = pl.DeviceIdType.MESH
CONTRACT_LAST = (((1,), (1,)), ((), ()))
CONTRACT_FIRST = (((0,), (0,)), ((), ()))


def kernel(
    n,
    rows,
    lengths,
    dest_rows,
    hidden,
    key_weight,
    value_weight,
    gain,
    freq,
    query,
    new_keys,
    new_values,
    out,
    hid_v,
    kw_v,
    vw_v,
    acc_k,
    acc_v,
    cos_v,
    sin_v,
    row_v,
    qbuf,
    o_send,
    s_send,
    o_recv,
    s_recv,
    near_k,
    near_v,
    mix_v,
    hid_sem,
    kw_sem,
    vw_sem,
    q_send_sem,
    q_recv_sem,
    o_send_sem,
    o_recv_sem,
    s_send_sem,
    s_recv_sem,
):
    me = lax.axis_index("ctx")
    my_row, my_head = me // KVH, me % KVH
    chunks, tok, depth = hid_v.shape
    nq = query.shape[1]
    scale = 1.0 / HD**0.5

    def chunk_copies(c):
        part = pl.ds(pl.multiple_of(c * depth, depth), depth)
        return (
            pltpu.make_async_copy(hidden.at[:, part], hid_v.at[c], hid_sem.at[c]),
            pltpu.make_async_copy(key_weight.at[part], kw_v.at[c], kw_sem.at[c]),
            pltpu.make_async_copy(value_weight.at[part], vw_v.at[c], vw_sem.at[c]),
        )

    barrier = pltpu.get_barrier_semaphore()

    @pl.loop(1, n)
    def _(i):
        pl.semaphore_signal(
            barrier, inc=1, device_id={"ctx": lax.rem(me + i, n)}, device_id_type=MESH
        )

    @pl.loop(0, chunks)
    def _(c):
        for copy in chunk_copies(c):
            copy.start()

    qbuf[my_head, my_row] = query[0]

    stream = me * tok + lax.broadcasted_iota(jnp.int32, (tok, LANES), 0)
    begin = jnp.int32(0)
    start_of = jnp.zeros((tok, LANES), jnp.int32)
    row_of = jnp.zeros((tok, LANES), jnp.int32)
    for p in range(rows):
        inside = stream >= begin
        start_of = jnp.where(inside, begin, start_of)
        row_of = jnp.where(inside, dest_rows[p], row_of)
        begin = begin + lengths[p]
    row_v[...] = row_of
    angle = (stream - start_of).astype(jnp.float32) * freq[...]
    cos_v[...] = jnp.cos(angle)
    sine = jnp.sin(angle)
    lane = lax.broadcasted_iota(jnp.int32, (tok, LANES), 1)
    sin_v[...] = jnp.where(lane < HD // 2, -sine, sine)

    pl.semaphore_wait(barrier, n - 1)

    def query_copy(d, s):
        return pltpu.make_async_remote_copy(
            src_ref=qbuf.at[my_head, my_row],
            dst_ref=qbuf.at[my_head, my_row],
            send_sem=q_send_sem.at[d],
            recv_sem=q_recv_sem.at[s],
            device_id={"ctx": d},
            device_id_type=MESH,
        )

    @pl.loop(1, n)
    def _(i):
        query_copy(lax.rem(me + i, n), me).start()

    steps = new_keys.shape[1]
    near_k[...] = jnp.zeros_like(near_k)
    near_v[...] = jnp.zeros_like(near_v)
    near_k[0:steps] = new_keys[0]
    near_v[0:steps] = new_values[0]
    own = jnp.concatenate([query[0]] * (LANES // nq), 0)
    near = lax.dot_general(near_k[...], own, CONTRACT_LAST, preferred_element_type=jnp.float32)
    near = near * scale
    u = lax.broadcasted_iota(jnp.int32, near.shape, 0)
    step_of = lax.broadcasted_iota(jnp.int32, near.shape, 1) % nq // QPK
    allowed = u <= jnp.minimum(step_of, steps - 1)
    near = jnp.where(allowed, near, NEG)
    near_top = jnp.max(near, 0, keepdims=True)
    near_w = jnp.where(allowed, jnp.exp(near - near_top), 0.0)
    near_sum = jnp.sum(near_w, 0, keepdims=True)
    near_o = lax.dot_general(
        near_w.astype(jnp.bfloat16), near_v[...], CONTRACT_FIRST, preferred_element_type=jnp.float32
    )[:nq]

    acc_k[...] = jnp.zeros_like(acc_k)
    acc_v[...] = jnp.zeros_like(acc_v)

    @pl.loop(0, chunks)
    def _(c):
        for copy in chunk_copies(c):
            copy.wait()
        h = hid_v[c]
        acc_k[...] += jnp.dot(h, kw_v[c], preferred_element_type=jnp.float32)
        acc_v[...] += jnp.dot(h, vw_v[c], preferred_element_type=jnp.float32)

    @pl.loop(1, n)
    def _(i):
        s = lax.rem(me + i, n)
        pltpu.make_async_remote_copy(
            src_ref=qbuf.at[my_head, my_row],
            dst_ref=qbuf.at[s % KVH, s // KVH],
            send_sem=q_send_sem.at[s],
            recv_sem=q_recv_sem.at[s],
            device_id={"ctx": s},
            device_id_type=MESH,
        ).wait_recv()

    def part_copies(r, h, d, s):
        return (
            pltpu.make_async_remote_copy(
                src_ref=o_send.at[h, r],
                dst_ref=o_recv.at[s],
                send_sem=o_send_sem.at[d],
                recv_sem=o_recv_sem.at[s],
                device_id={"ctx": d},
                device_id_type=MESH,
            ),
            pltpu.make_async_remote_copy(
                src_ref=s_send.at[h, r * nq // LANES],
                dst_ref=s_recv.at[s],
                send_sem=s_send_sem.at[d],
                recv_sem=s_recv_sem.at[s],
                device_id={"ctx": d},
                device_id_type=MESH,
            ),
        )

    wide = rows * nq
    column_row = lax.broadcasted_iota(jnp.int32, (tok, wide), 1) // nq
    row_of = jnp.concatenate([row_v[...]] * (wide // LANES), 1)
    live = row_of == column_row
    for h in range(KVH):
        cols = slice(h * HD, (h + 1) * HD)
        raw = acc_k[:, cols]
        normed = raw * lax.rsqrt(jnp.mean(raw * raw, -1, keepdims=True) + EPS) * gain[...]
        keys = normed * cos_v[...] + pltpu.roll(normed, HD // 2, 1) * sin_v[...]
        values = acc_v[:, cols].astype(jnp.bfloat16)
        far = lax.dot_general(
            keys.astype(jnp.bfloat16),
            qbuf[h].reshape(wide, HD),
            CONTRACT_LAST,
            preferred_element_type=jnp.float32,
        )
        far = jnp.where(live, far * scale, NEG)
        top = jnp.max(far, 0, keepdims=True)
        weights = jnp.where(live, jnp.exp(far - top), 0.0)
        total = jnp.sum(weights, 0, keepdims=True)
        mixed = lax.dot_general(
            weights.astype(jnp.bfloat16), values, CONTRACT_FIRST, preferred_element_type=jnp.float32
        )
        o_send[h] = mixed.astype(jnp.bfloat16).reshape(rows, nq, HD)
        for b in range(wide // LANES):
            block = slice(b * LANES, (b + 1) * LANES)
            s_send[h, b] = jnp.concatenate([top[:, block], total[:, block]], 0)

        @pl.loop(0, rows)
        def _(i):
            r = lax.rem(my_row + i, rows)
            d = r * KVH + h

            @pl.when(d != me)
            def _():
                for copy in part_copies(r, h, d, me):
                    copy.start()

    o_recv[me] = o_send[my_head, my_row]
    s_recv[me] = s_send[my_head, my_row * nq // LANES]

    @pl.loop(1, n)
    def _(i):
        s = lax.rem(me + i, n)
        for copy in part_copies(s // KVH, s % KVH, s, s):
            copy.wait_recv()

    tops, sums = s_recv[:, 0, :], s_recv[:, 1, :]
    best = jnp.maximum(jnp.max(tops, 0, keepdims=True), near_top)
    factor = jnp.exp(tops - best)
    near_factor = jnp.exp(near_top - best)
    total = jnp.sum(factor * sums, 0, keepdims=True) + near_factor * near_sum
    shares = jnp.concatenate(
        [
            factor / total,
            near_factor / total,
            jnp.zeros((LANES - n - 1, LANES), jnp.float32),
        ],
        0,
    )
    mix_v[...] = shares.T
    mine = mix_v[pl.ds(pl.multiple_of(lax.rem(my_row * nq, LANES), nq), nq), :]
    result = near_o * mine[:, n : n + 1]
    for s in range(n):
        result = result + o_recv[s].astype(jnp.float32) * mine[:, s : s + 1]
    out[0] = result.astype(jnp.bfloat16)

    @pl.loop(1, n)
    def _(i):
        d = lax.rem(me + i, n)
        query_copy(d, me).wait_send()
        for copy in part_copies(d // KVH, d % KVH, d, me):
            copy.wait_send()


def local(
    hidden, key_weight, value_weight, key_gain, lengths, dest_rows, queries, new_keys, new_values
):
    n = lax.axis_size("ctx")
    rows = lengths.shape[0]
    tok, width = hidden.shape
    nq = queries.shape[1]
    kv = KVH * HD
    depth = 512
    chunks = width // depth
    half = np.arange(HD // 2, dtype=np.float32)
    freq = np.power(np.float32(ROPE_BASE), np.float32(-2.0) * half / np.float32(HD))
    freq = jnp.asarray(np.concatenate([freq, freq])[None, :].astype(np.float32))
    vmem = pl.BlockSpec(memory_space=pltpu.VMEM)
    smem = pl.BlockSpec(memory_space=pltpu.SMEM)
    hbm = pl.BlockSpec(memory_space=pl.ANY)
    bf16, f32 = jnp.bfloat16, jnp.float32
    blocks = rows * nq // LANES
    return pl.pallas_call(
        functools.partial(kernel, n, rows),
        out_shape=jax.ShapeDtypeStruct((1, nq, HD), bf16),
        in_specs=[smem, smem, hbm, hbm, hbm, vmem, vmem, vmem, vmem, vmem],
        out_specs=vmem,
        scratch_shapes=[
            pltpu.VMEM((chunks, tok, depth), bf16),
            pltpu.VMEM((chunks, depth, kv), bf16),
            pltpu.VMEM((chunks, depth, kv), bf16),
            pltpu.VMEM((tok, kv), f32),
            pltpu.VMEM((tok, kv), f32),
            pltpu.VMEM((tok, LANES), f32),
            pltpu.VMEM((tok, LANES), f32),
            pltpu.VMEM((tok, LANES), jnp.int32),
            pltpu.VMEM((KVH, rows, nq, HD), bf16),
            pltpu.VMEM((KVH, rows, nq, HD), bf16),
            pltpu.VMEM((KVH, blocks, 2, LANES), f32),
            pltpu.VMEM((n, nq, HD), bf16),
            pltpu.VMEM((n, 2, LANES), f32),
            pltpu.VMEM((16, HD), bf16),
            pltpu.VMEM((16, HD), bf16),
            pltpu.VMEM((LANES, LANES), f32),
            pltpu.SemaphoreType.DMA((chunks,)),
            pltpu.SemaphoreType.DMA((chunks,)),
            pltpu.SemaphoreType.DMA((chunks,)),
            pltpu.SemaphoreType.DMA((n,)),
            pltpu.SemaphoreType.DMA((n,)),
            pltpu.SemaphoreType.DMA((n,)),
            pltpu.SemaphoreType.DMA((n,)),
            pltpu.SemaphoreType.DMA((n,)),
            pltpu.SemaphoreType.DMA((n,)),
        ],
        compiler_params=pltpu.CompilerParams(
            collective_id=0, has_side_effects=True, vmem_limit_bytes=40 * 1024 * 1024
        ),
    )(
        lengths,
        dest_rows,
        hidden,
        key_weight,
        value_weight,
        key_gain[None, :],
        freq,
        queries,
        new_keys,
        new_values,
    )


def solution(mesh):
    placed = (
        P(("groups", "ctx"), None),
        P(),
        P(),
        P(),
        P("groups"),
        P("groups"),
        P(("groups", "ctx"), None, None),
        P(("groups", "ctx"), None, None),
        P(("groups", "ctx"), None, None),
    )
    return jax.shard_map(
        local,
        mesh=mesh,
        in_specs=placed,
        out_specs=P(("groups", "ctx"), None, None),
        check_vma=False,
    )
```

```python
import functools

import jax
import jax.numpy as jnp
import numpy as np
from jax import lax
from jax.experimental import pallas as pl
from jax.experimental.pallas import tpu as pltpu
from jax.sharding import PartitionSpec as P

KVH = 4
HD = 128
QPK = 8
HALF = KVH // 2
LANES = 128

ROPE_BASE = 1000000.0
EPS = 1e-06
NEG = -1e30
MESH = pl.DeviceIdType.MESH
CONTRACT_LAST = (((1,), (1,)), ((), ()))
CONTRACT_FIRST = (((0,), (0,)), ((), ()))


def kernel(
    n,
    rows,
    early,
    lengths_hbm,
    dest_hbm,
    hidden,
    key_weight,
    value_weight,
    gain_hbm,
    freq_hbm,
    query_hbm,
    new_keys_hbm,
    new_values_hbm,
    out,
    lengths,
    dest_rows,
    gain,
    freq,
    query,
    new_keys,
    new_values,
    hid_v,
    kw_v,
    vw_v,
    acc_k,
    acc_v,
    cos_v,
    sin_v,
    row_v,
    qbuf,
    k_send,
    v_send,
    k_all,
    v_all,
    o_send,
    s_send,
    o_recv,
    s_recv,
    near_k,
    near_v,
    mix_v,
    small_sem,
    hid_sem,
    kw_sem,
    vw_sem,
    q_send_sem,
    q_recv_sem,
    kv_send_sem,
    kv_recv_sem,
    o_send_sem,
    o_recv_sem,
    s_send_sem,
    s_recv_sem,
):
    me = lax.axis_index("ctx")
    core, chip = lax.rem(me, 2), me // 2
    sibling = me + 1 - 2 * core
    chips = n // 2
    my_row, my_k = chip // HALF, lax.rem(chip, HALF)
    chunks, tok, depth = hid_v.shape
    nq = query.shape[1]
    scale = 1.0 / HD**0.5
    wide = rows * nq

    def chunk_copies(c):
        part = pl.ds(pl.multiple_of(c * depth, depth), depth)
        return (
            pltpu.make_async_copy(hidden.at[:, part], hid_v.at[c], hid_sem.at[c]),
            pltpu.make_async_copy(key_weight.at[part], kw_v.at[c], kw_sem.at[c]),
            pltpu.make_async_copy(value_weight.at[part], vw_v.at[c], vw_sem.at[c]),
        )

    def remote(src, dst, send_sem, recv_sem, device):
        return pltpu.make_async_remote_copy(
            src_ref=src,
            dst_ref=dst,
            send_sem=send_sem,
            recv_sem=recv_sem,
            device_id={"ctx": device},
            device_id_type=MESH,
        )

    def query_copy(other, source):
        slot = qbuf.at[lax.rem(source, HALF), source // HALF]
        return remote(
            qbuf.at[my_k, my_row],
            slot,
            q_send_sem.at[other],
            q_recv_sem.at[source],
            other * 2 + core,
        )

    def part_copies(k, r, source):
        other = r * HALF + k
        device = other * 2 + core
        return (
            remote(
                o_send.at[k, r],
                o_recv.at[source],
                o_send_sem.at[other],
                o_recv_sem.at[source],
                device,
            ),
            remote(
                s_send.at[k, r * nq // LANES],
                s_recv.at[source],
                s_send_sem.at[other],
                s_recv_sem.at[source],
                device,
            ),
        )

    key_copies = [
        remote(k_send.at[k], k_all.at[k, 1], kv_send_sem.at[k], kv_recv_sem.at[k], sibling)
        for k in range(HALF)
    ]
    value_copies = [
        remote(
            v_send.at[k],
            v_all.at[k, 1],
            kv_send_sem.at[HALF + k],
            kv_recv_sem.at[HALF + k],
            sibling,
        )
        for k in range(HALF)
    ]

    small = [
        pltpu.make_async_copy(src, dst, small_sem.at[i])
        for i, (src, dst) in enumerate(
            [
                (lengths_hbm, lengths),
                (dest_hbm, dest_rows),
                (freq_hbm, freq),
                (query_hbm, query),
                (gain_hbm, gain),
                (new_keys_hbm, new_keys),
                (new_values_hbm, new_values),
            ]
        )
    ]
    for copy in small:
        copy.start()

    barrier = pltpu.get_barrier_semaphore()

    @pl.loop(1, chips)
    def _(i):
        pl.semaphore_signal(
            barrier,
            inc=1,
            device_id={"ctx": lax.rem(chip + i, chips) * 2 + core},
            device_id_type=MESH,
        )

    pl.semaphore_signal(barrier, inc=1, device_id={"ctx": sibling}, device_id_type=MESH)

    @pl.loop(0, chunks)
    def _(c):
        for copy in chunk_copies(c):
            copy.start()

    for copy in small:
        copy.wait()
    qbuf[my_k, my_row] = query[0]

    count = lax.broadcasted_iota(jnp.int32, (tok, LANES), 0)
    lane = lax.broadcasted_iota(jnp.int32, (tok, LANES), 1)
    for side, device in enumerate((me, sibling)):
        stream = device * tok + count
        begin = jnp.int32(0)
        start_of = jnp.zeros((tok, LANES), jnp.int32)
        row_of = jnp.zeros((tok, LANES), jnp.int32)
        for p in range(rows):
            inside = stream >= begin
            if side == 0:
                start_of = jnp.where(inside, begin, start_of)
            row_of = jnp.where(inside, dest_rows[p], row_of)
            begin = begin + lengths[p]
        row_v[side] = row_of
        if side == 0:
            angle = (stream - start_of).astype(jnp.float32) * freq[...]
            cos_v[...] = jnp.cos(angle)
            sine = jnp.sin(angle)
            sin_v[...] = jnp.where(lane < HD // 2, -sine, sine)

    steps = new_keys.shape[1]
    near_k[...] = jnp.zeros_like(near_k)
    near_v[...] = jnp.zeros_like(near_v)
    near_k[0:steps] = new_keys[0]
    near_v[0:steps] = new_values[0]
    own = jnp.concatenate([query[0]] * (LANES // nq), 0)
    near = lax.dot_general(near_k[...], own, CONTRACT_LAST, preferred_element_type=jnp.float32)
    near = near * scale
    u = lax.broadcasted_iota(jnp.int32, near.shape, 0)
    step_of = lax.broadcasted_iota(jnp.int32, near.shape, 1) % nq // QPK
    allowed = u <= jnp.minimum(step_of, steps - 1)
    near = jnp.where(allowed, near, NEG)
    near_top = jnp.max(near, 0, keepdims=True)
    near_w = jnp.where(allowed, jnp.exp(near - near_top), 0.0)
    near_sum = jnp.sum(near_w, 0, keepdims=True)
    near_o = lax.dot_general(
        near_w.astype(jnp.bfloat16), near_v[...], CONTRACT_FIRST, preferred_element_type=jnp.float32
    )[:nq]

    acc_k[...] = jnp.zeros_like(acc_k)
    acc_v[...] = jnp.zeros_like(acc_v)

    def project(c):
        for copy in chunk_copies(c):
            copy.wait()
        h = hid_v[c]
        acc_k[...] += jnp.dot(h, kw_v[c], preferred_element_type=jnp.float32)
        acc_v[...] += jnp.dot(h, vw_v[c], preferred_element_type=jnp.float32)

    pl.loop(0, early)(project)
    pl.semaphore_wait(barrier, chips)

    @pl.loop(1, chips)
    def _(i):
        query_copy(lax.rem(chip + i, chips), chip).start()

    pl.loop(early, chunks)(project)

    def columns(k, side):
        head = 2 * k + (core if side == 0 else 1 - core)
        return pl.ds(pl.multiple_of(head * HD, HD), HD)

    def make_keys(k, side):
        raw = acc_k[:, columns(k, side)]
        normed = raw * lax.rsqrt(jnp.mean(raw * raw, -1, keepdims=True) + EPS) * gain[...]
        keys = normed * cos_v[...] + pltpu.roll(normed, HD // 2, 1) * sin_v[...]
        return keys.astype(jnp.bfloat16)

    for k in range(HALF):
        k_send[k] = make_keys(k, 1)
        key_copies[k].start()
    for k in range(HALF):
        v_send[k] = acc_v[:, columns(k, 1)].astype(jnp.bfloat16)
        value_copies[k].start()
    for k in range(HALF):
        k_all[k, 0] = make_keys(k, 0)
        v_all[k, 0] = acc_v[:, columns(k, 0)].astype(jnp.bfloat16)

    @pl.loop(1, chips)
    def _(i):
        other = lax.rem(chip + i, chips)
        query_copy(other, other).wait_recv()

    column_row = lax.broadcasted_iota(jnp.int32, (2 * tok, wide), 1) // nq
    row_of = jnp.concatenate([row_v[...].reshape(2 * tok, LANES)] * (wide // LANES), 1)
    live = row_of == column_row
    for k in range(HALF):
        key_copies[k].wait_recv()
        far = lax.dot_general(
            k_all[k].reshape(2 * tok, HD),
            qbuf[k].reshape(wide, HD),
            CONTRACT_LAST,
            preferred_element_type=jnp.float32,
        )
        far = jnp.where(live, far * scale, NEG)
        top = jnp.max(far, 0, keepdims=True)
        weights = jnp.where(live, jnp.exp(far - top), 0.0)
        total = jnp.sum(weights, 0, keepdims=True)
        value_copies[k].wait_recv()
        mixed = lax.dot_general(
            weights.astype(jnp.bfloat16),
            v_all[k].reshape(2 * tok, HD),
            CONTRACT_FIRST,
            preferred_element_type=jnp.float32,
        )
        o_send[k] = mixed.astype(jnp.bfloat16).reshape(rows, nq, HD)
        for b in range(wide // LANES):
            block = slice(b * LANES, (b + 1) * LANES)
            s_send[k, b] = jnp.concatenate([top[:, block], total[:, block]], 0)

        @pl.loop(0, rows)
        def _(i):
            r = lax.rem(my_row + i, rows)

            @pl.when(r * HALF + k != chip)
            def _():
                for copy in part_copies(k, r, chip):
                    copy.start()

    o_recv[chip] = o_send[my_k, my_row]
    s_recv[chip] = s_send[my_k, my_row * nq // LANES]

    @pl.loop(1, chips)
    def _(i):
        other = lax.rem(chip + i, chips)
        for copy in part_copies(lax.rem(other, HALF), other // HALF, other):
            copy.wait_recv()

    tops, sums = s_recv[:, 0, :], s_recv[:, 1, :]
    best = jnp.maximum(jnp.max(tops, 0, keepdims=True), near_top)
    factor = jnp.exp(tops - best)
    near_factor = jnp.exp(near_top - best)
    total = jnp.sum(factor * sums, 0, keepdims=True) + near_factor * near_sum
    shares = jnp.concatenate(
        [
            factor / total,
            near_factor / total,
            jnp.zeros((LANES - chips - 1, LANES), jnp.float32),
        ],
        0,
    )
    mix_v[...] = shares.T
    mine = mix_v[pl.ds(pl.multiple_of(lax.rem(my_row * nq, LANES), nq), nq), :]
    result = near_o * mine[:, chips : chips + 1]
    for s in range(chips):
        result = result + o_recv[s].astype(jnp.float32) * mine[:, s : s + 1]
    out[0] = result.astype(jnp.bfloat16)

    for copy in key_copies + value_copies:
        copy.wait_send()

    @pl.loop(1, chips)
    def _(i):
        other = lax.rem(chip + i, chips)
        query_copy(other, chip).wait_send()
        for copy in part_copies(lax.rem(other, HALF), other // HALF, chip):
            copy.wait_send()


def local(
    hidden, key_weight, value_weight, key_gain, lengths, dest_rows, queries, new_keys, new_values
):
    n = lax.axis_size("ctx")
    chips = n // 2
    rows = lengths.shape[0]
    tok, width = hidden.shape
    nq = queries.shape[1]
    kv = KVH * HD
    depth = 512
    chunks = width // depth
    half = np.arange(HD // 2, dtype=np.float32)
    freq = np.power(np.float32(ROPE_BASE), np.float32(-2.0) * half / np.float32(HD))
    freq = jnp.asarray(np.concatenate([freq, freq])[None, :].astype(np.float32))
    vmem = pl.BlockSpec(memory_space=pltpu.VMEM)
    hbm = pl.BlockSpec(memory_space=pltpu.HBM)
    bf16, f32 = jnp.bfloat16, jnp.float32
    blocks = rows * nq // LANES
    return pl.pallas_call(
        functools.partial(kernel, n, rows, chunks // 2),
        out_shape=jax.ShapeDtypeStruct((1, nq, HD), bf16),
        in_specs=[hbm] * 10,
        out_specs=vmem,
        scratch_shapes=[
            pltpu.SMEM((rows,), jnp.int32),
            pltpu.SMEM((rows,), jnp.int32),
            pltpu.VMEM((1, HD), f32),
            pltpu.VMEM((1, LANES), f32),
            pltpu.VMEM((1, nq, HD), bf16),
            pltpu.VMEM(new_keys.shape, bf16),
            pltpu.VMEM(new_values.shape, bf16),
            pltpu.VMEM((chunks, tok, depth), bf16),
            pltpu.VMEM((chunks, depth, kv), bf16),
            pltpu.VMEM((chunks, depth, kv), bf16),
            pltpu.VMEM((tok, kv), f32),
            pltpu.VMEM((tok, kv), f32),
            pltpu.VMEM((tok, LANES), f32),
            pltpu.VMEM((tok, LANES), f32),
            pltpu.VMEM((2, tok, LANES), jnp.int32),
            pltpu.VMEM((HALF, rows, nq, HD), bf16),
            pltpu.VMEM((HALF, tok, HD), bf16),
            pltpu.VMEM((HALF, tok, HD), bf16),
            pltpu.VMEM((HALF, 2, tok, HD), bf16),
            pltpu.VMEM((HALF, 2, tok, HD), bf16),
            pltpu.VMEM((HALF, rows, nq, HD), bf16),
            pltpu.VMEM((HALF, blocks, 2, LANES), f32),
            pltpu.VMEM((chips, nq, HD), bf16),
            pltpu.VMEM((chips, 2, LANES), f32),
            pltpu.VMEM((16, HD), bf16),
            pltpu.VMEM((16, HD), bf16),
            pltpu.VMEM((LANES, LANES), f32),
            pltpu.SemaphoreType.DMA((7,)),
            pltpu.SemaphoreType.DMA((chunks,)),
            pltpu.SemaphoreType.DMA((chunks,)),
            pltpu.SemaphoreType.DMA((chunks,)),
            pltpu.SemaphoreType.DMA((chips,)),
            pltpu.SemaphoreType.DMA((chips,)),
            pltpu.SemaphoreType.DMA((KVH,)),
            pltpu.SemaphoreType.DMA((KVH,)),
            pltpu.SemaphoreType.DMA((chips,)),
            pltpu.SemaphoreType.DMA((chips,)),
            pltpu.SemaphoreType.DMA((chips,)),
            pltpu.SemaphoreType.DMA((chips,)),
        ],
        compiler_params=pltpu.CompilerParams(
            collective_id=0, has_side_effects=True, vmem_limit_bytes=60 * 1024 * 1024
        ),
    )(
        lengths,
        dest_rows,
        hidden,
        key_weight,
        value_weight,
        key_gain[None, :],
        freq,
        queries,
        new_keys,
        new_values,
    )


def solution(mesh):
    placed = (
        P(("groups", "ctx"), None),
        P(),
        P(),
        P(),
        P("groups"),
        P("groups"),
        P(("groups", "ctx"), None, None),
        P(("groups", "ctx"), None, None),
        P(("groups", "ctx"), None, None),
    )
    return jax.shard_map(
        local,
        mesh=mesh,
        in_specs=placed,
        out_specs=P(("groups", "ctx"), None, None),
        check_vma=False,
    )
```

```python
import functools

import jax
import jax.numpy as jnp
import numpy as np
from jax import lax
from jax.experimental import pallas as pl
from jax.experimental.pallas import tpu as pltpu
from jax.sharding import PartitionSpec as P

KVH = 4
HD = 128
QPK = 8
HALF = KVH // 2
LANES = 128

ROPE_BASE = 1000000.0
EPS = 1e-06
NEG = -1e30
MESH = pl.DeviceIdType.MESH
CONTRACT_LAST = (((1,), (1,)), ((), ()))
CONTRACT_FIRST = (((0,), (0,)), ((), ()))


def kernel(
    n,
    rows,
    early,
    ahead,
    lengths_hbm,
    dest_hbm,
    hidden,
    key_weight,
    value_weight,
    gain_hbm,
    freq_hbm,
    query_hbm,
    new_keys_hbm,
    new_values_hbm,
    out,
    lengths,
    dest_rows,
    gain,
    freq,
    query,
    new_keys,
    new_values,
    hid_v,
    kw_v,
    vw_v,
    acc_k,
    acc_v,
    cos_v,
    sin_v,
    row_v,
    qbuf,
    k_send,
    v_send,
    k_all,
    v_all,
    o_send,
    s_send,
    o_recv,
    s_recv,
    near_k,
    near_v,
    mix_v,
    small_sem,
    hid_sem,
    kw_sem,
    vw_sem,
    q_send_sem,
    q_recv_sem,
    kv_send_sem,
    kv_recv_sem,
    o_send_sem,
    o_recv_sem,
    s_send_sem,
    s_recv_sem,
):
    me = lax.axis_index("ctx")
    core, chip = lax.rem(me, 2), me // 2
    sibling = me + 1 - 2 * core
    chips = n // 2
    my_row, my_k = chip // HALF, lax.rem(chip, HALF)
    chunks, tok, depth = hid_v.shape
    nq = query.shape[1]
    scale = 1.0 / HD**0.5
    wide = rows * nq

    def chunk_copies(c):
        part = pl.ds(pl.multiple_of(c * depth, depth), depth)
        return (
            pltpu.make_async_copy(hidden.at[:, part], hid_v.at[c], hid_sem.at[c]),
            pltpu.make_async_copy(key_weight.at[part], kw_v.at[c], kw_sem.at[c]),
            pltpu.make_async_copy(value_weight.at[part], vw_v.at[c], vw_sem.at[c]),
        )

    def remote(src, dst, send_sem, recv_sem, device):
        return pltpu.make_async_remote_copy(
            src_ref=src,
            dst_ref=dst,
            send_sem=send_sem,
            recv_sem=recv_sem,
            device_id={"ctx": device},
            device_id_type=MESH,
        )

    def query_copy(other, source):
        slot = qbuf.at[lax.rem(source, HALF), source // HALF]
        return remote(
            qbuf.at[my_k, my_row],
            slot,
            q_send_sem.at[other],
            q_recv_sem.at[source],
            other * 2 + core,
        )

    def part_copies(k, r, source):
        other = r * HALF + k
        device = other * 2 + core
        return (
            remote(
                o_send.at[k, r],
                o_recv.at[source],
                o_send_sem.at[other],
                o_recv_sem.at[source],
                device,
            ),
            remote(
                s_send.at[k, r * nq // LANES],
                s_recv.at[source],
                s_send_sem.at[other],
                s_recv_sem.at[source],
                device,
            ),
        )

    key_copies = [
        remote(k_send.at[k], k_all.at[k, 1], kv_send_sem.at[k], kv_recv_sem.at[k], sibling)
        for k in range(HALF)
    ]
    value_copies = [
        remote(
            v_send.at[k],
            v_all.at[k, 1],
            kv_send_sem.at[HALF + k],
            kv_recv_sem.at[HALF + k],
            sibling,
        )
        for k in range(HALF)
    ]

    small = [
        pltpu.make_async_copy(src, dst, small_sem.at[i])
        for i, (src, dst) in enumerate(
            [
                (lengths_hbm, lengths),
                (dest_hbm, dest_rows),
                (freq_hbm, freq),
                (query_hbm, query),
                (gain_hbm, gain),
                (new_keys_hbm, new_keys),
                (new_values_hbm, new_values),
            ]
        )
    ]
    barrier = pltpu.get_barrier_semaphore()

    @pl.loop(1, chips)
    def _(i):
        pl.semaphore_signal(
            barrier,
            inc=1,
            device_id={"ctx": lax.rem(chip + i, chips) * 2 + core},
            device_id_type=MESH,
        )

    pl.semaphore_signal(barrier, inc=1, device_id={"ctx": sibling}, device_id_type=MESH)

    for copy in small:
        copy.start()

    @pl.loop(0, min(ahead, chunks))
    def _(c):
        for copy in chunk_copies(c):
            copy.start()

    for copy in small:
        copy.wait()
    qbuf[my_k, my_row] = query[0]

    span = min(-(-tok // (8 * chunks)) * 8, tok)
    count = lax.broadcasted_iota(jnp.int32, (span, LANES), 0)
    lane = lax.broadcasted_iota(jnp.int32, (span, LANES), 1)

    def tables(c):
        first = pl.multiple_of(jnp.minimum(c * span, tok - span), 8)
        place = pl.ds(first, span)
        mine, theirs = (device * tok + first + count for device in (me, sibling))
        begin = jnp.int32(0)
        start_of = jnp.zeros((span, LANES), jnp.int32)
        my_rows = jnp.zeros((span, LANES), jnp.int32)
        their_rows = jnp.zeros((span, LANES), jnp.int32)
        for p in range(rows):
            inside = mine >= begin
            start_of = jnp.where(inside, begin, start_of)
            my_rows = jnp.where(inside, dest_rows[p], my_rows)
            their_rows = jnp.where(theirs >= begin, dest_rows[p], their_rows)
            begin = begin + lengths[p]
        row_v[0, place] = my_rows
        row_v[1, place] = their_rows
        angle = (mine - start_of).astype(jnp.float32) * freq[...]
        cos_v[place] = jnp.cos(angle)
        sine = jnp.sin(angle)
        sin_v[place] = jnp.where(lane < HD // 2, -sine, sine)

    acc_k[...] = jnp.zeros_like(acc_k)
    acc_v[...] = jnp.zeros_like(acc_v)

    def project(c):
        for copy in chunk_copies(c):
            copy.wait()

        @pl.when(c + ahead < chunks)
        def _():
            for copy in chunk_copies(c + ahead):
                copy.start()

        tables(c)
        h = hid_v[c]
        acc_k[...] += jnp.dot(h, kw_v[c], preferred_element_type=jnp.float32)
        acc_v[...] += jnp.dot(h, vw_v[c], preferred_element_type=jnp.float32)

    pl.loop(0, early)(project)
    pl.semaphore_wait(barrier, chips)

    @pl.loop(1, chips)
    def _(i):
        query_copy(lax.rem(chip + i, chips), chip).start()

    pl.loop(early, chunks)(project)

    def columns(k, side):
        head = 2 * k + (core if side == 0 else 1 - core)
        return pl.ds(pl.multiple_of(head * HD, HD), HD)

    def make_keys(k, side):
        raw = acc_k[:, columns(k, side)]
        normed = raw * lax.rsqrt(jnp.mean(raw * raw, -1, keepdims=True) + EPS) * gain[...]
        keys = normed * cos_v[...] + pltpu.roll(normed, HD // 2, 1) * sin_v[...]
        return keys.astype(jnp.bfloat16)

    for k in range(HALF):
        k_send[k] = make_keys(k, 1)
        key_copies[k].start()
    for k in range(HALF):
        v_send[k] = acc_v[:, columns(k, 1)].astype(jnp.bfloat16)
        value_copies[k].start()
    for k in range(HALF):
        k_all[k, 0] = make_keys(k, 0)
        v_all[k, 0] = acc_v[:, columns(k, 0)].astype(jnp.bfloat16)

    @pl.loop(1, chips)
    def _(i):
        other = lax.rem(chip + i, chips)
        query_copy(other, other).wait_recv()

    column_row = lax.broadcasted_iota(jnp.int32, (2 * tok, wide), 1) // nq
    row_of = jnp.concatenate([row_v[...].reshape(2 * tok, LANES)] * (wide // LANES), 1)
    live = row_of == column_row
    for k in range(HALF):
        key_copies[k].wait_recv()
        far = lax.dot_general(
            k_all[k].reshape(2 * tok, HD),
            qbuf[k].reshape(wide, HD),
            CONTRACT_LAST,
            preferred_element_type=jnp.float32,
        )
        far = jnp.where(live, far * scale, NEG)
        top = jnp.max(far, 0, keepdims=True)
        weights = jnp.where(live, jnp.exp(far - top), 0.0)
        total = jnp.sum(weights, 0, keepdims=True)
        value_copies[k].wait_recv()
        mixed = lax.dot_general(
            weights.astype(jnp.bfloat16),
            v_all[k].reshape(2 * tok, HD),
            CONTRACT_FIRST,
            preferred_element_type=jnp.float32,
        )
        o_send[k] = mixed.astype(jnp.bfloat16).reshape(rows, nq, HD)
        for b in range(wide // LANES):
            block = slice(b * LANES, (b + 1) * LANES)
            s_send[k, b] = jnp.concatenate([top[:, block], total[:, block]], 0)

        @pl.loop(0, rows)
        def _(i):
            r = lax.rem(my_row + i, rows)

            @pl.when(r * HALF + k != chip)
            def _():
                for copy in part_copies(k, r, chip):
                    copy.start()

    steps = new_keys.shape[1]
    near_k[...] = jnp.zeros_like(near_k)
    near_v[...] = jnp.zeros_like(near_v)
    near_k[0:steps] = new_keys[0]
    near_v[0:steps] = new_values[0]
    own = jnp.concatenate([query[0]] * (LANES // nq), 0)
    near = lax.dot_general(near_k[...], own, CONTRACT_LAST, preferred_element_type=jnp.float32)
    near = near * scale
    u = lax.broadcasted_iota(jnp.int32, near.shape, 0)
    step_of = lax.broadcasted_iota(jnp.int32, near.shape, 1) % nq // QPK
    allowed = u <= jnp.minimum(step_of, steps - 1)
    near = jnp.where(allowed, near, NEG)
    near_top = jnp.max(near, 0, keepdims=True)
    near_w = jnp.where(allowed, jnp.exp(near - near_top), 0.0)
    near_sum = jnp.sum(near_w, 0, keepdims=True)
    near_o = lax.dot_general(
        near_w.astype(jnp.bfloat16), near_v[...], CONTRACT_FIRST, preferred_element_type=jnp.float32
    )[:nq]

    o_recv[chip] = o_send[my_k, my_row]
    s_recv[chip] = s_send[my_k, my_row * nq // LANES]

    for copy in key_copies + value_copies:
        copy.wait_send()

    @pl.loop(1, chips)
    def _(i):
        other = lax.rem(chip + i, chips)
        query_copy(other, chip).wait_send()
        for copy in part_copies(lax.rem(other, HALF), other // HALF, chip):
            copy.wait_send()

    @pl.loop(1, chips)
    def _(i):
        other = lax.rem(chip + i, chips)
        for copy in part_copies(lax.rem(other, HALF), other // HALF, other):
            copy.wait_recv()

    tops, sums = s_recv[:, 0, :], s_recv[:, 1, :]
    best = jnp.maximum(jnp.max(tops, 0, keepdims=True), near_top)
    factor = jnp.exp(tops - best)
    near_factor = jnp.exp(near_top - best)
    total = jnp.sum(factor * sums, 0, keepdims=True) + near_factor * near_sum
    shares = jnp.concatenate(
        [
            factor / total,
            near_factor / total,
            jnp.zeros((LANES - chips - 1, LANES), jnp.float32),
        ],
        0,
    )
    mix_v[...] = shares.T
    mine = mix_v[pl.ds(pl.multiple_of(lax.rem(my_row * nq, LANES), nq), nq), :]
    result = near_o * mine[:, chips : chips + 1]
    for s in range(chips):
        result = result + o_recv[s].astype(jnp.float32) * mine[:, s : s + 1]
    out[0] = result.astype(jnp.bfloat16)


def local(
    hidden, key_weight, value_weight, key_gain, lengths, dest_rows, queries, new_keys, new_values
):
    n = lax.axis_size("ctx")
    chips = n // 2
    rows = lengths.shape[0]
    tok, width = hidden.shape
    nq = queries.shape[1]
    kv = KVH * HD
    depth = 512
    chunks = width // depth
    half = np.arange(HD // 2, dtype=np.float32)
    freq = np.power(np.float32(ROPE_BASE), np.float32(-2.0) * half / np.float32(HD))
    freq = jnp.asarray(np.concatenate([freq, freq])[None, :].astype(np.float32))
    vmem = pl.BlockSpec(memory_space=pltpu.VMEM)
    hbm = pl.BlockSpec(memory_space=pltpu.HBM)
    bf16, f32 = jnp.bfloat16, jnp.float32
    blocks = rows * nq // LANES
    return pl.pallas_call(
        functools.partial(kernel, n, rows, 4, 4),
        out_shape=jax.ShapeDtypeStruct((1, nq, HD), bf16),
        in_specs=[hbm] * 10,
        out_specs=vmem,
        scratch_shapes=[
            pltpu.SMEM((rows,), jnp.int32),
            pltpu.SMEM((rows,), jnp.int32),
            pltpu.VMEM((1, HD), f32),
            pltpu.VMEM((1, LANES), f32),
            pltpu.VMEM((1, nq, HD), bf16),
            pltpu.VMEM(new_keys.shape, bf16),
            pltpu.VMEM(new_values.shape, bf16),
            pltpu.VMEM((chunks, tok, depth), bf16),
            pltpu.VMEM((chunks, depth, kv), bf16),
            pltpu.VMEM((chunks, depth, kv), bf16),
            pltpu.VMEM((tok, kv), f32),
            pltpu.VMEM((tok, kv), f32),
            pltpu.VMEM((tok, LANES), f32),
            pltpu.VMEM((tok, LANES), f32),
            pltpu.VMEM((2, tok, LANES), jnp.int32),
            pltpu.VMEM((HALF, rows, nq, HD), bf16),
            pltpu.VMEM((HALF, tok, HD), bf16),
            pltpu.VMEM((HALF, tok, HD), bf16),
            pltpu.VMEM((HALF, 2, tok, HD), bf16),
            pltpu.VMEM((HALF, 2, tok, HD), bf16),
            pltpu.VMEM((HALF, rows, nq, HD), bf16),
            pltpu.VMEM((HALF, blocks, 2, LANES), f32),
            pltpu.VMEM((chips, nq, HD), bf16),
            pltpu.VMEM((chips, 2, LANES), f32),
            pltpu.VMEM((16, HD), bf16),
            pltpu.VMEM((16, HD), bf16),
            pltpu.VMEM((LANES, LANES), f32),
            pltpu.SemaphoreType.DMA((7,)),
            pltpu.SemaphoreType.DMA((chunks,)),
            pltpu.SemaphoreType.DMA((chunks,)),
            pltpu.SemaphoreType.DMA((chunks,)),
            pltpu.SemaphoreType.DMA((chips,)),
            pltpu.SemaphoreType.DMA((chips,)),
            pltpu.SemaphoreType.DMA((KVH,)),
            pltpu.SemaphoreType.DMA((KVH,)),
            pltpu.SemaphoreType.DMA((chips,)),
            pltpu.SemaphoreType.DMA((chips,)),
            pltpu.SemaphoreType.DMA((chips,)),
            pltpu.SemaphoreType.DMA((chips,)),
        ],
        compiler_params=pltpu.CompilerParams(
            collective_id=0, has_side_effects=True, vmem_limit_bytes=60 * 1024 * 1024
        ),
    )(
        lengths,
        dest_rows,
        hidden,
        key_weight,
        value_weight,
        key_gain[None, :],
        freq,
        queries,
        new_keys,
        new_values,
    )


def solution(mesh):
    placed = (
        P(("groups", "ctx"), None),
        P(),
        P(),
        P(),
        P("groups"),
        P("groups"),
        P(("groups", "ctx"), None, None),
        P(("groups", "ctx"), None, None),
        P(("groups", "ctx"), None, None),
    )
    return jax.shard_map(
        local,
        mesh=mesh,
        in_specs=placed,
        out_specs=P(("groups", "ctx"), None, None),
        check_vma=False,
    )
```
